512 devices in a mesh: gx: 32 (over z_lo, y, core), gy: 16 (over z_hi, x).
Axes of the slice: x: 4, y: 8, z: 8 (z_hi: 4, z_lo: 2; z = z_hi * 2 + z_lo), core: 2. Of those that a mesh axis runs over, the one named last changes fastest.
Arguments:
- node_feats: bfloat16 [32, 16, 128, 64], P('gx', 'gy'), may hold values from -6 to 6
- positions: float32 [32, 16, 3, 64], P('gx', 'gy'), may hold values from 0 to 50, as said below
- species: int32 [32, 16, 64], P('gx', 'gy'), may hold values from 0 to 9
- occupied: int32 [32, 16, 64], P('gx', 'gy'), may hold values 0 or 1
- energy_shift: float32 [10], replicated, may hold values from -4 to 4
- energy_scale: float32 [10], replicated, may hold values from 0.1 to 1.9
- radial_weight: float32 [4, 3, 128], replicated, may hold values from -1.8 to 1.8
- mix_weight: bfloat16 [384, 128], replicated, may hold values from -0.3125 to 0.3125
- readout: float32 [128], replicated, may hold values from -0.5 to 0.5
Outputs:
- atom_energy: float32 [32, 16, 64], P('gx', 'gy')
- forces: float32 [32, 16, 3, 64], P('gx', 'gy')
- feature_grad: float32 [32, 16, 128, 64], P('gx', 'gy')
The draws below stay inside these ranges and needn't reach their ends.
Inputs may be any that keep to these rules, and one draw needn't show every extreme that they name: `positions`: each coordinate is measured from its own cell's corner, the first two along the grid's dimensions (up to 5), the third across the slab (up to 50); no two slots lie closer than 0.9.
All inputs are finite; a program needn't handle non-finite values. No bound on the sum of `occupied` on one device may be relied on, other than what follows from the above.
Results may differ from the reference program's by a relative error of at most 0.0046.
Values may be sent and summed in bfloat16 or wider, within the bound.
A program may use at most 64 MiB of HBM per device.

```python
import math
from functools import partial
import jax
import jax.numpy as jnp
from jax import lax

C = 128
NB = 4
SLOTS = 64
SPEC = 10
NCX = 32
NCY = 16


def cell_order(cell_key):
    return jax.random.permutation(cell_key, SLOTS)


def draw_positions(key, part):
    key = jax.random.fold_in(key, 7)
    order_key = jax.random.fold_in(key, 2)
    first_key = jax.random.fold_in(key, 3)
    second_key = jax.random.fold_in(key, 4)
    height_key = jax.random.fold_in(key, 5)
    cell_keys = jax.random.split(order_key, NCX * NCY)
    layer_index = jax.vmap(cell_order)(cell_keys).reshape(NCX, NCY, SLOTS)
    parity = (layer_index % 2).astype(jnp.float32)
    first_unit = jax.random.uniform(first_key, (NCX, NCY, SLOTS), jnp.float32, 0.0, 1.0)
    second_unit = jax.random.uniform(second_key, (NCX, NCY, SLOTS), jnp.float32, 0.0, 1.0)
    height_jitter = jax.random.uniform(height_key, (NCX, NCY, SLOTS), jnp.float32, -0.1, 0.1)
    first_coord = 0.45 + 2.4 * parity + 1.7 * first_unit
    second_coord = 0.45 + 4.1 * second_unit
    layer_gap = 50.0 / SLOTS
    third_coord = (layer_index.astype(jnp.float32) + 0.5) * layer_gap + height_jitter
    return jnp.stack([first_coord, second_coord, third_coord], axis=2)


def touch_ends(result, key, smallest, top_value):
    longest = result.shape.index(max(result.shape))
    spots = []
    for shift in (0, 1):
        where = [jax.random.randint(jax.random.fold_in(key, axis), (), 0, length) for axis, length in enumerate(result.shape)]
        where[longest] = (where[longest] + shift) % result.shape[longest]
        spots.append(tuple(where))
    return result.at[spots[0]].set(smallest).at[spots[1]].set(top_value)


def block_levels(rng, shape, cuts, low, high):
    level = 1.0
    for dim, blocks in cuts:
        draws = jax.random.uniform(jax.random.fold_in(jax.random.fold_in(rng, 6), dim), (blocks,), jnp.float32, low / len(cuts), high / len(cuts))
        level = level * jnp.repeat(jnp.exp(draws), shape[dim] // blocks).reshape((-1,) + (1,) * (len(shape) - 1 - dim))
    return level


def gaussian(rng, shape, deviation, most, cuts=(), kind=jnp.bfloat16):
    level = block_levels(rng, shape, cuts, -0.22, 0.18) if cuts else 1.0
    values = jax.random.normal(rng, shape, jnp.float32) * deviation * level
    return jnp.minimum(jnp.maximum(values, -most), most).astype(kind)


def setup_inputs(seed: int = 0) -> dict:
    splits = jax.random.split(jax.random.key(seed), 10)
    node_feats = gaussian(splits[0], (NCX, NCY, C, SLOTS), 1.0, 6.0, ((0, 32), (1, 16)))
    positions = draw_positions(jax.random.fold_in(splits[9], 71), 0)
    species = touch_ends(jax.random.randint(splits[2], (NCX, NCY, SLOTS), 0, SPEC), jax.random.fold_in(splits[2], 1), 0, SPEC - 1).astype(jnp.int32)
    occupied = touch_ends((jax.random.randint(splits[3], (NCX, NCY, SLOTS), 0, 16) < 15).astype(jnp.int32), jax.random.fold_in(splits[3], 1), 0, 1)
    energy_shift = gaussian(splits[4], (SPEC,), 1.0, 4.0, (), jnp.float32)
    energy_scale = jnp.clip(1.0 + 0.18 * jax.random.normal(splits[5], (SPEC,), jnp.float32), 0.1, 1.9)
    radial_weight = gaussian(splits[6], (NB, 3, C), 0.3, 1.8, (), jnp.float32)
    mix_weight = gaussian(splits[7], (3 * C, C), (3 * C) ** -0.5, 0.3125)
    readout = gaussian(splits[8], (C,), C ** -0.5, 0.5, (), jnp.float32)
    return dict(node_feats=node_feats, positions=positions, species=species, occupied=occupied, energy_shift=energy_shift, energy_scale=energy_scale, radial_weight=radial_weight, mix_weight=mix_weight, readout=readout)


CELL_SIDE = 5.0
CUTOFF = 5.0
OFFSET_LIST = tuple(((step_x, step_y) for step_x in (-1, 0, 1) for step_y in (-1, 0, 1)))

def pair_basis(centre_pos, other_pos, shift_x, shift_y, same_cell):
    float_kind = centre_pos.dtype
    slot_count = centre_pos.shape[1]
    offset = jnp.array([shift_x * CELL_SIDE, shift_y * CELL_SIDE, 0.0], float_kind)
    relative = other_pos[:, None, :] - centre_pos[:, :, None] + offset[:, None, None]
    dist_sq = lax.optimization_barrier(jnp.sum(relative * relative, axis=0))
    if same_cell:
        self_pair = jnp.eye(slot_count, dtype=float_kind)
        dist_sq = dist_sq + self_pair
        keep_pair = 1.0 - self_pair
    else:
        keep_pair = jnp.ones_like(dist_sq)
    distance = jnp.sqrt(dist_sq)
    unit_vec = relative / distance
    scaled = distance / CUTOFF
    poly = 1.0 - 28.0 * scaled ** 6 + 48.0 * scaled ** 7 - 21.0 * scaled ** 8
    envelope = jnp.where(scaled < 1.0, poly, 0.0) * keep_pair
    orders = jnp.arange(1, NB + 1).astype(float_kind)[:, None, None]
    radial = math.sqrt(2.0 / CUTOFF) * jnp.sin(orders * math.pi * scaled) / distance * envelope
    unit_x, unit_y, unit_z = (unit_vec[0], unit_vec[1], unit_vec[2])
    root_three = math.sqrt(3.0)
    root_fifteen = math.sqrt(15.0)
    harmonic = jnp.stack([jnp.ones_like(unit_x), root_three * unit_x, root_three * unit_y, root_three * unit_z, root_fifteen * unit_x * unit_y, root_fifteen * unit_y * unit_z, 0.5 * math.sqrt(5.0) * (3.0 * unit_z * unit_z - 1.0), root_fifteen * unit_x * unit_z, 0.5 * root_fifteen * (unit_x * unit_x - unit_y * unit_y)])
    return (radial[:, None] * harmonic[None]).reshape(-1, slot_count, slot_count)

def expand_radial(radial_weight):
    return jnp.concatenate([radial_weight[:, 0:1], jnp.repeat(radial_weight[:, 1:2], 3, axis=1), jnp.repeat(radial_weight[:, 2:3], 5, axis=1)], axis=1)

def to_bf16_and_back(value):
    return lax.optimization_barrier(value.astype(jnp.bfloat16)).astype(jnp.float32)

def messages(centre_pos, near_pos, near_feat, picks):
    total = None
    for number, shift_x, shift_y in picks:
        basis = pair_basis(centre_pos, near_pos[number], shift_x, shift_y, shift_x == 0 and shift_y == 0)
        term = jnp.einsum('kij,cj->kic', to_bf16_and_back(basis), near_feat[number].astype(jnp.float32))
        total = term if total is None else total + term
    return total

def cell_tail(total, centre_pos, species_row, mask_row, near_pos, near_feat, energy_shift, energy_scale, radial_weight, mix_weight, readout):
    channels = readout.shape[0]
    slot_count = centre_pos.shape[1]
    wide = expand_radial(radial_weight)
    split = total.reshape(wide.shape[0], 9, slot_count, channels)
    amp = lax.optimization_barrier(jnp.sum(wide[:, :, None, :] * split, axis=0))
    invariants = jnp.concatenate([amp[0], lax.optimization_barrier(jnp.sum(amp[1:4] * amp[1:4], axis=0)), lax.optimization_barrier(jnp.sum(amp[4:9] * amp[4:9], axis=0))], axis=1).astype(jnp.bfloat16)
    pre = jnp.dot(invariants, mix_weight, preferred_element_type=jnp.float32)
    sigma = jax.nn.sigmoid(pre)
    onehot = (species_row[:, None] == jnp.arange(energy_shift.shape[0], dtype=jnp.int32)[None, :]).astype(jnp.float32)
    shift_row = lax.optimization_barrier(jnp.sum(onehot * energy_shift[None, :], axis=1))
    scale_row = lax.optimization_barrier(jnp.sum(onehot * energy_scale[None, :], axis=1))
    mask_float = mask_row.astype(jnp.float32)
    energy = mask_float * (shift_row + scale_row * lax.optimization_barrier(jnp.sum(pre * sigma * readout[None, :], axis=1)))
    coef = mask_float * scale_row
    dpre = (coef[:, None] * readout[None, :] * sigma * (1.0 + pre * (1.0 - sigma))).astype(jnp.bfloat16)
    dinv = jnp.dot(dpre, mix_weight.T, preferred_element_type=jnp.float32)
    damp = jnp.concatenate([dinv[None, :, :channels], 2.0 * amp[1:4] * dinv[None, :, channels:2 * channels], 2.0 * amp[4:9] * dinv[None, :, 2 * channels:]], axis=0)
    coeff = to_bf16_and_back((wide[:, :, None, :] * damp[None]).reshape(-1, slot_count, channels))
    grad_centre = jnp.zeros((3, slot_count), jnp.float32)
    pieces = []
    for number, (shift_x, shift_y) in enumerate(OFFSET_LIST):
        local_basis = partial(pair_basis, shift_x=shift_x, shift_y=shift_y, same_cell=shift_x == 0 and shift_y == 0)
        basis, pull_back = jax.vjp(local_basis, centre_pos, near_pos[number])
        dbasis = jnp.einsum('kic,cj->kij', coeff, near_feat[number].astype(jnp.float32))
        grad_i, grad_j = pull_back(dbasis)
        dfeat = jnp.einsum('kij,kic->cj', to_bf16_and_back(basis), coeff)
        grad_centre = grad_centre + grad_i
        pieces.append(jnp.concatenate([dfeat, grad_j], axis=0))
    return (energy, grad_centre, jnp.stack(pieces))

def neighbours(padded, cells_x, cells_y):
    stacked = jnp.stack([padded[1 + step_x:1 + step_x + cells_x, 1 + step_y:1 + step_y + cells_y] for step_x, step_y in OFFSET_LIST], axis=2)
    return stacked.reshape((cells_x * cells_y, len(OFFSET_LIST)) + padded.shape[2:])

def reference(node_feats, positions, species, occupied, energy_shift, energy_scale, radial_weight, mix_weight, readout):
    grid_x, grid_y, channels, slot_count = node_feats.shape
    mask_float = occupied.astype(jnp.float32)
    masked = (node_feats.astype(jnp.float32) * mask_float[:, :, None, :]).astype(jnp.bfloat16)
    widths = ((1, 1), (1, 1), (0, 0), (0, 0))
    near_feat = neighbours(jnp.pad(masked, widths, mode='wrap'), grid_x, grid_y)
    near_pos = neighbours(jnp.pad(positions, widths, mode='wrap'), grid_x, grid_y)
    picks = tuple(((number, shift_x, shift_y) for number, (shift_x, shift_y) in enumerate(OFFSET_LIST)))
    cell_total = grid_x * grid_y

    def per_cell(inputs):
        centre_pos, species_row, mask_row, cell_pos, cell_feat = inputs
        total = messages(centre_pos, cell_pos, cell_feat, picks)
        return cell_tail(total, centre_pos, species_row, mask_row, cell_pos, cell_feat, energy_shift, energy_scale, radial_weight, mix_weight, readout)
    energy, grad_centre, pieces = lax.map(per_cell, (positions.reshape(cell_total, 3, slot_count), species.reshape(cell_total, slot_count), occupied.reshape(cell_total, slot_count), near_pos, near_feat))
    pieces = pieces.reshape(grid_x, grid_y, len(OFFSET_LIST), channels + 3, slot_count)
    gathered = jnp.zeros((grid_x + 2, grid_y + 2, channels + 3, slot_count), jnp.float32)
    for number, (shift_x, shift_y) in enumerate(OFFSET_LIST):
        gathered = gathered.at[1 + shift_x:1 + shift_x + grid_x, 1 + shift_y:1 + shift_y + grid_y].add(pieces[:, :, number])
    gathered = gathered.at[:, 1].add(gathered[:, -1])
    gathered = gathered.at[:, -2].add(gathered[:, 0])
    gathered = gathered.at[1, 1:-1].add(gathered[-1, 1:-1])
    gathered = gathered.at[-2, 1:-1].add(gathered[0, 1:-1])
    owned = gathered[1:-1, 1:-1]
    forces = -(grad_centre.reshape(grid_x, grid_y, 3, slot_count) + owned[:, :, channels:])
    feature_grad = owned[:, :, :channels] * mask_float[:, :, None, :]
    return (energy.reshape(grid_x, grid_y, slot_count), forces, feature_grad)
```

```python
import math

import jax
import jax.numpy as jnp
from jax import lax
from jax.experimental import pallas as pl
from jax.experimental.pallas import tpu as pltpu
from jax.sharding import PartitionSpec as P

NB = 4
SIDE = 5.0
OFFSETS = ((-1, -1), (-1, 0), (-1, 1), (0, -1), (0, 1), (1, -1), (1, 0), (1, 1))
DEGREE = (0, 1, 1, 1, 2, 2, 2, 2, 2)
S, C, K = 64, 128, 36
LANES = 640
FAR = 1.0e4

SIN_POLY = (0.9999999535014531, -4.934792863930696, 4.058412034401939, -1.331881022938153, 0.21969869886953738)
COS_POLY = (3.1415925800860727, -5.167706881428528, 2.5500314173387735, -0.5980454081793043, 0.07722057976690203)
R3, R5, R15 = math.sqrt(3.0), math.sqrt(5.0), math.sqrt(15.0)
F32, BF16 = jnp.float32, jnp.bfloat16


def poly(coefs, x):
    total = coefs[-1]
    for coef in coefs[-2::-1]:
        total = total * x + coef
    return total


def geometry(centre, other, eye):
    rx, ry, rz = (o - c for o, c in zip(other, centre))
    dist_sq = rx * rx + ry * ry + rz * rz
    if eye is not None:
        dist_sq = dist_sq + eye
    rinv = lax.rsqrt(dist_sq)
    x = jnp.minimum(dist_sq * rinv * (1.0 / SIDE), 1.0)
    y = x - 0.5
    y2 = y * y
    s1 = poly(SIN_POLY, y2)
    c1 = -y * poly(COS_POLY, y2)
    x2 = x * x
    x5 = x2 * x2 * x
    env = 1.0 + x5 * x * (-28.0 + x * (48.0 - 21.0 * x))
    denv = x5 * (-168.0 + x * (336.0 - 168.0 * x))
    norm = math.sqrt(2.0 / SIDE)
    kinv = norm * rinv
    if eye is not None:
        kinv = kinv * (1.0 - eye)
    g = env * kinv
    dg = denv * kinv * (1.0 / SIDE) - g * rinv
    t = 2.0 * c1
    sines = [s1, t * s1]
    cosines = [c1, t * c1 - 1.0]
    for _ in range(NB - 2):
        sines.append(t * sines[-1] - sines[-2])
        cosines.append(t * cosines[-1] - cosines[-2])
    radial = [g * s for s in sines]
    dradial = [dg * s + (g * ((n + 1) * math.pi / SIDE)) * c for n, (s, c) in enumerate(zip(sines, cosines))]
    return radial, dradial, (rx * rinv, ry * rinv, rz * rinv), rinv


def harmonics(u):
    ux, uy, uz = u
    ax, ay, az = R3 * ux, R3 * uy, R3 * uz
    bx, by = R5 * ax, R5 * ay
    return (
        None,
        ax,
        ay,
        az,
        bx * uy,
        by * uz,
        (1.5 * R5) * (uz * uz) - 0.5 * R5,
        bx * uz,
        0.5 * (bx * ux - by * uy),
    )


def kernel(
    nf_h, pos_h, spec_h, occ_h, esh_h, esc_h, rw_h, mix_h, ro_h,
    energy_o, force_o, fgrad_o,
    nf, pos, spec, occ, esh, esc, rw, mix, ro,
    feat, posb, rows, cols, basis, geo, dbs, coeff, pieces, gsend, precv, grecv, giacc,
    ps_sem, pr_sem, fs_sem, fr_sem, ds_sem, dr_sem, gs_sem, gr_sem, in_sem,
):
    sources = (pos_h, occ_h, nf_h, spec_h, esh_h, esc_h, rw_h, mix_h, ro_h)
    targets = (pos, occ, nf, spec, esh, esc, rw, mix, ro)
    loads = [pltpu.make_async_copy(a, b, in_sem.at[i]) for i, (a, b) in enumerate(zip(sources, targets))]
    for load in loads:
        load.start()

    nx, ny = lax.axis_size("gx"), lax.axis_size("gy")
    mx, my = lax.axis_index("gx"), lax.axis_index("gy")

    def device(slot):
        p, q = OFFSETS[slot]
        return (lax.rem(mx + p + nx, nx), lax.rem(my + q + ny, ny))

    def remote(src, dst, send, recv, slot):
        return pltpu.make_async_remote_copy(
            src_ref=src, dst_ref=dst, send_sem=send, recv_sem=recv,
            device_id=device(slot), device_id_type=pl.DeviceIdType.MESH,
        )

    barrier = pltpu.get_barrier_semaphore()
    for slot in range(8):
        pl.semaphore_signal(barrier, inc=1, device_id=device(slot), device_id_type=pl.DeviceIdType.MESH)

    for load in loads[:3]:
        load.wait()
    occ_row = occ[0].astype(F32)
    own = jnp.concatenate([pos[0, a] for a in range(3)] + [occ_row, jnp.zeros((4, S), F32)], axis=0)
    own = jnp.concatenate([own, own], axis=1)
    posb[8] = own
    columns = own.T
    occ_col = columns[0:S, 3:4]
    feat[pl.ds(8 * S, S), :] = nf[0, 0] * occ_col.astype(BF16)
    feat[pl.ds(9 * S, S), :] = jnp.zeros((S, C), BF16)

    pl.semaphore_wait(barrier, 8)
    pos_copies = [remote(posb.at[8], posb.at[7 - s], ps_sem.at[s], pr_sem.at[7 - s], s) for s in range(8)]
    feat_copies = [
        remote(feat.at[pl.ds(8 * S, S)], feat.at[pl.ds((7 - s) * S, S)], fs_sem.at[s], fr_sem.at[7 - s], s)
        for s in range(8)
    ]
    for copy in pos_copies:
        copy.start()
    for copy in feat_copies:
        copy.start()

    for load in loads[3:]:
        load.wait()
    species = spec[0]
    shift_row = jnp.zeros((1, S), F32)
    scale_row = jnp.zeros((1, S), F32)
    for kind in range(esh.shape[0]):
        hit = species == kind
        shift_row = jnp.where(hit, esh[kind], shift_row)
        scale_row = jnp.where(hit, esc[kind], scale_row)
    low = lax.broadcasted_iota(jnp.int32, (1, C), 1) < S
    for a in range(3):
        cols[a] = jnp.broadcast_to(columns[0:S, a : a + 1], (S, C))
    scale_tile = jnp.concatenate([scale_row, jnp.zeros((7, S), F32)], axis=0)
    scale_col = jnp.concatenate([scale_tile, scale_tile], axis=1).T[0:S, 0:1]
    coef_col = occ_col * scale_col

    def pair_tile(tile, own_tile):
        lanes = pl.ds(tile * C, C)

        def body(ib, carry):
            at = pl.ds(pl.multiple_of(ib * 16, 16), 16)
            centre = [cols[a, at, :] for a in range(3)]
            other = [rows[a : a + 1, lanes] for a in range(3)]
            eye = None
            if own_tile:
                sub = lax.broadcasted_iota(jnp.int32, (16, C), 0) + ib * 16
                eye = (sub == lax.broadcasted_iota(jnp.int32, (16, C), 1)).astype(F32)
            radial, dradial, u, rinv = geometry(centre, other, eye)
            for n in range(NB):
                geo[n, at, lanes] = radial[n]
                geo[NB + n, at, lanes] = dradial[n]
            for a in range(3):
                geo[2 * NB + a, at, lanes] = u[a]
            geo[2 * NB + 3, at, lanes] = rinv
            ys = harmonics(u)
            for n in range(NB):
                for lm in range(9):
                    value = radial[n] if lm == 0 else radial[n] * ys[lm]
                    basis[pl.ds(pl.multiple_of((n * 9 + lm) * S + ib * 16, 16), 16), lanes] = value.astype(BF16)
            return carry

        lax.fori_loop(0, 4, body, 0)

    for a in range(3):
        rows[a : a + 1, pl.ds(4 * C, C)] = jnp.where(low, posb[8, a : a + 1, :], FAR)
    pair_tile(4, True)

    for s in range(8):
        pos_copies[s].wait_recv()
    for tile in range(4):
        first, second = OFFSETS[2 * tile], OFFSETS[2 * tile + 1]
        for a in range(3):
            pair = jnp.where(low, posb[2 * tile, a : a + 1, :], posb[2 * tile + 1, a : a + 1, :])
            if a < 2:
                pair = pair + jnp.where(low, SIDE * first[a], SIDE * second[a])
            rows[a : a + 1, pl.ds(tile * C, C)] = pair
        pair_tile(tile, False)

    for s in range(8):
        feat_copies[s].wait_recv()
    sums = jnp.dot(basis[...], feat[...], preferred_element_type=F32)
    weight = [[rw[d, n : n + 1, :] for d in range(3)] for n in range(NB)]
    amp = []
    for lm in range(9):
        total = None
        for n in range(NB):
            k = n * 9 + lm
            term = weight[n][DEGREE[lm]] * sums[k * S : (k + 1) * S]
            total = term if total is None else total + term
        amp.append(total)
    second = amp[1] * amp[1] + amp[2] * amp[2] + amp[3] * amp[3]
    third = amp[4] * amp[4] + amp[5] * amp[5] + amp[6] * amp[6] + amp[7] * amp[7] + amp[8] * amp[8]
    invariants = jnp.concatenate([amp[0].astype(BF16), second.astype(BF16), third.astype(BF16)], axis=1)
    pre = jnp.dot(invariants, mix[...], preferred_element_type=F32)
    sigma = jax.nn.sigmoid(pre)
    readout = ro[...]
    dpre = (coef_col * readout * sigma * (1.0 + pre * (1.0 - sigma))).astype(BF16)
    dinv = lax.dot_general(dpre, mix[...], (((1,), (1,)), ((), ())), preferred_element_type=F32)
    for lm in range(9):
        d = DEGREE[lm]
        damp = dinv[:, d * C : (d + 1) * C]
        if d > 0:
            damp = 2.0 * amp[lm] * damp
        for n in range(NB):
            coeff[pl.ds((n * 9 + lm) * S, S), :] = (weight[n][d] * damp).astype(BF16)

    piece_copies = []
    for half in range(2):
        part = lax.dot_general(
            coeff[...], basis[:, pl.ds(half * 2 * C, 2 * C)], (((0,), (0,)), ((), ())), preferred_element_type=F32
        ).T.astype(BF16)
        for i in range(4):
            s = half * 4 + i
            pieces[s] = part[i * S : (i + 1) * S]
            copy = remote(pieces.at[s], precv.at[7 - s], ds_sem.at[s], dr_sem.at[7 - s], s)
            copy.start()
            piece_copies.append(copy)
    own_part = lax.dot_general(
        coeff[...], basis[:, pl.ds(4 * C, C)], (((0,), (0,)), ((), ())), preferred_element_type=F32
    )

    energy_row = jnp.sum((pre * sigma * readout).T, axis=0, keepdims=True)
    energy_o[0] = occ_row * (shift_row + scale_row * energy_row)

    def force_tile(tile, column):
        lanes = pl.ds(tile * C, C)

        def body(ib, carry):
            at = pl.ds(pl.multiple_of(ib * 16, 16), 16)
            radial = [geo[n, at, lanes] for n in range(NB)]
            dradial = [geo[NB + n, at, lanes] for n in range(NB)]
            u = [geo[2 * NB + a, at, lanes] for a in range(3)]
            rinv = geo[2 * NB + 3, at, lanes]
            ys = harmonics(u)
            along = [None] * NB
            across = [None] * 9
            for n in range(NB):
                for lm in range(9):
                    value = dbs[pl.ds(pl.multiple_of((n * 9 + lm) * S + ib * 16, 16), 16), pl.ds(column, C)]
                    term = value if lm == 0 else value * ys[lm]
                    along[n] = term if along[n] is None else along[n] + term
                    if lm:
                        term = radial[n] * value
                        across[lm] = term if across[lm] is None else across[lm] + term
            outward = along[0] * dradial[0]
            for n in range(1, NB):
                outward = outward + along[n] * dradial[n]
            e = across
            ux, uy, uz = u
            vx = R3 * e[1] + R15 * (uy * e[4] + uz * e[7] + ux * e[8])
            vy = R3 * e[2] + R15 * (ux * e[4] + uz * e[5] - uy * e[8])
            vz = R3 * e[3] + R15 * (uy * e[5] + ux * e[7]) + (3.0 * R5) * (uz * e[6])
            radial_part = outward - rinv * (ux * vx + uy * vy + uz * vz)
            sums_j = []
            for a, v in enumerate((vx, vy, vz)):
                grad = rinv * v + u[a] * radial_part
                if tile == 0:
                    giacc[a, at, :] = grad
                else:
                    giacc[a, at, :] = giacc[a, at, :] + grad
                sums_j.append(carry[a] + grad[0:8] + grad[8:16])
            return tuple(sums_j)

        zero = jnp.zeros((8, C), F32)
        totals = lax.fori_loop(0, 4, body, (zero, zero, zero))
        return jnp.concatenate(
            [jnp.sum(t, axis=0, keepdims=True) for t in totals] + [jnp.zeros((5, C), F32)], axis=0
        )

    grad_copies = []
    for half in range(2):
        dbs[...] = lax.dot_general(
            coeff[...], feat[pl.ds(half * 4 * S, 4 * S), :], (((1,), (1,)), ((), ())), preferred_element_type=F32
        )
        for i in range(2):
            tile = half * 2 + i
            gsend[tile] = force_tile(tile, i * C)
            for s in (2 * tile, 2 * tile + 1):
                copy = remote(gsend.at[tile], grecv.at[7 - s], gs_sem.at[s], gr_sem.at[7 - s], s)
                copy.start()
                grad_copies.append(copy)
    dbs[:, pl.ds(0, C)] = lax.dot_general(
        coeff[...], feat[pl.ds(8 * S, 2 * S), :], (((1,), (1,)), ((), ())), preferred_element_type=F32
    )
    own_grad = force_tile(4, 0)
    centre_rows = [jnp.sum(giacc[a].T, axis=0, keepdims=True) for a in range(3)]

    for s in range(8):
        piece_copies[s].wait_recv()
    gathered = precv[0].astype(F32)
    for s in range(1, 8):
        gathered = gathered + precv[s].astype(F32)
    fgrad_o[0, 0] = (gathered + own_part.T[:S, :]) * occ_col

    for s in range(8):
        grad_copies[s].wait_recv()
    upper = grecv[0] + grecv[2] + grecv[4] + grecv[6]
    lower = grecv[1] + grecv[3] + grecv[5] + grecv[7] + own_grad
    back = lower[0:3, 0:S] + upper[0:3, S:C]
    for a in range(3):
        force_o[0, a] = centre_rows[a] - back[a : a + 1]

    for copies in (pos_copies, feat_copies, piece_copies, grad_copies):
        for copy in copies:
            copy.wait_send()


def emit(a, b, c, ao, bo, co, sem):
    copies = [pltpu.make_async_copy(x, y, sem.at[i]) for i, (x, y) in enumerate(((a, ao), (b, bo), (c, co)))]
    for copy in copies:
        copy.start()
    for copy in copies:
        copy.wait()


def shards(nf, pos, spec, occ, esh, esc, rw, mix, ro):
    vmem = pl.BlockSpec(memory_space=pltpu.VMEM)
    hbm = pl.BlockSpec(memory_space=pltpu.HBM)
    dma = pltpu.SemaphoreType.DMA((8,))
    shapes = (
        jax.ShapeDtypeStruct((1, 1, S), F32),
        jax.ShapeDtypeStruct((1, 3, 1, S), F32),
        jax.ShapeDtypeStruct((1, 1, S, C), F32),
    )
    inputs = (nf.swapaxes(2, 3), pos.swapaxes(1, 2), spec, occ, esh, esc, rw.swapaxes(0, 1), mix, ro.reshape(1, C))
    results = pl.pallas_call(
        kernel,
        out_shape=shapes,
        in_specs=[hbm] * 9,
        out_specs=(vmem, vmem, vmem),
        scratch_shapes=[
            pltpu.VMEM((1, 1, S, C), BF16),
            pltpu.VMEM((1, 3, 1, S), F32),
            pltpu.VMEM((1, 1, S), jnp.int32),
            pltpu.VMEM((1, 1, S), jnp.int32),
            pltpu.SMEM(esh.shape, F32),
            pltpu.SMEM(esh.shape, F32),
            pltpu.VMEM((3, NB, C), F32),
            pltpu.VMEM((3 * C, C), BF16),
            pltpu.VMEM((1, C), F32),
            pltpu.VMEM((LANES, C), BF16),
            pltpu.VMEM((9, 8, C), F32),
            pltpu.VMEM((8, LANES), F32),
            pltpu.VMEM((3, S, C), F32),
            pltpu.VMEM((K * S, LANES), BF16),
            pltpu.VMEM((3 * NB, S, LANES), F32),
            pltpu.VMEM((K * S, 2 * C), F32),
            pltpu.VMEM((K * S, C), BF16),
            pltpu.VMEM((8, S, C), BF16),
            pltpu.VMEM((4, 8, C), F32),
            pltpu.VMEM((8, S, C), BF16),
            pltpu.VMEM((8, 8, C), F32),
            pltpu.VMEM((3, S, C), F32),
            dma, dma, dma, dma, dma, dma, dma, dma,
            pltpu.SemaphoreType.DMA((9,)),
        ],
        compiler_params=pltpu.CompilerParams(
            collective_id=0, has_side_effects=True, vmem_limit_bytes=48 * 1024 * 1024
        ),
        cost_estimate=pl.CostEstimate(flops=1_100_000_000, bytes_accessed=400_000, transcendentals=100_000),
    )(*[pltpu.with_memory_space_constraint(v, pltpu.HBM) for v in inputs])
    energy, forces, fgrad = pl.pallas_call(
        emit,
        out_shape=shapes,
        in_specs=[vmem] * 3,
        out_specs=(hbm,) * 3,
        scratch_shapes=[pltpu.SemaphoreType.DMA((3,))],
    )(*results)
    return energy, forces.swapaxes(1, 2), fgrad.swapaxes(2, 3)


def solution(mesh):
    placed = (
        P("gx", "gy", None, None),
        P("gx", "gy", None, None),
        P("gx", "gy", None),
        P("gx", "gy", None),
        P(), P(), P(), P(), P(),
    )
    return jax.shard_map(
        shards,
        mesh=mesh,
        in_specs=placed,
        out_specs=(P("gx", "gy", None), P("gx", "gy", None, None), P("gx", "gy", None, None)),
        check_vma=False,
    )
```

```python
import math

import jax
import jax.numpy as jnp
from jax import lax
from jax.experimental import pallas as pl
from jax.experimental.pallas import tpu as pltpu
from jax.sharding import PartitionSpec as P

NB = 4
SIDE = 5.0
OFFSETS = ((-1, 1), (1, 1), (0, 1), (1, 0), (-1, -1), (1, -1), (0, -1), (-1, 0))
OPPOSITE = (5, 4, 6, 7, 1, 0, 2, 3)
MIRROR = (1, 0, 2, 7, 5, 4, 6, 3)
DEGREE = (0, 1, 1, 1, 2, 2, 2, 2, 2)
S, C, K = 64, 128, 36
LANES = 640
FAR = 1.0e4

SIN_POLY = (0.9999999535014531, -4.934792863930696, 4.058412034401939, -1.331881022938153, 0.21969869886953738)
COS_POLY = (3.1415925800860727, -5.167706881428528, 2.5500314173387735, -0.5980454081793043, 0.07722057976690203)
R3, R5, R15 = math.sqrt(3.0), math.sqrt(5.0), math.sqrt(15.0)
F32, BF16 = jnp.float32, jnp.bfloat16


def poly(coefs, x):
    total = coefs[-1]
    for coef in coefs[-2::-1]:
        total = total * x + coef
    return total


def geometry(centre, other, eye):
    rx, ry, rz = (o - c for o, c in zip(other, centre))
    dist_sq = rx * rx + ry * ry + rz * rz
    if eye is not None:
        dist_sq = dist_sq + eye
    rinv = lax.rsqrt(dist_sq)
    x = jnp.minimum(dist_sq * rinv * (1.0 / SIDE), 1.0)
    y = x - 0.5
    y2 = y * y
    s1 = poly(SIN_POLY, y2)
    c1 = -y * poly(COS_POLY, y2)
    x2 = x * x
    x5 = x2 * x2 * x
    env = 1.0 + x5 * x * (-28.0 + x * (48.0 - 21.0 * x))
    denv = x5 * (-168.0 + x * (336.0 - 168.0 * x))
    norm = math.sqrt(2.0 / SIDE)
    kinv = norm * rinv
    if eye is not None:
        kinv = kinv * (1.0 - eye)
    g = env * kinv
    dg = denv * kinv * (1.0 / SIDE) - g * rinv
    t = 2.0 * c1
    sines = [s1, t * s1]
    cosines = [c1, t * c1 - 1.0]
    for _ in range(NB - 2):
        sines.append(t * sines[-1] - sines[-2])
        cosines.append(t * cosines[-1] - cosines[-2])
    radial = [g * s for s in sines]
    dradial = [dg * s + (g * ((n + 1) * math.pi / SIDE)) * c for n, (s, c) in enumerate(zip(sines, cosines))]
    return radial, dradial, (rx * rinv, ry * rinv, rz * rinv), rinv


def harmonics(u):
    ux, uy, uz = u
    ax, ay, az = R3 * ux, R3 * uy, R3 * uz
    bx, by = R5 * ax, R5 * ay
    return (
        None,
        ax,
        ay,
        az,
        bx * uy,
        by * uz,
        (1.5 * R5) * (uz * uz) - 0.5 * R5,
        bx * uz,
        0.5 * (bx * ux - by * uy),
    )


def kernel(
    nf_h, pos_h, spec_h, occ_h, esh_h, esc_h, rw_h, mix_h, ro_h,
    energy_o, force_o, fgrad_o,
    nf, pos, spec, occ, esh, esc, rw, mix, ro,
    feat, posb, rows, cols, basis, geo, dbs, coeff, coeff_t, near, pieces, gsend, precv, grecv, giacc,
    ps_sem, pr_sem, fs_sem, fr_sem, ds_sem, dr_sem, gs_sem, gr_sem, in_sem,
):
    nx, ny = lax.axis_size("gx"), lax.axis_size("gy")
    mx, my = lax.axis_index("gx"), lax.axis_index("gy")

    inner = lax.div(my + ny - 1, ny)
    flip = 2 * inner - 1

    def device(slot):
        p, q = OFFSETS[slot]
        return (lax.rem(mx + p + nx, nx), lax.rem(my + q * flip + ny, ny))

    def landing(slot):
        if OFFSETS[slot][1] == 0:
            return OPPOSITE[slot]
        other = lax.div(device(slot)[1] + ny - 1, ny)
        mixed = inner + other - 2 * inner * other
        return OPPOSITE[slot] + mixed * (MIRROR[slot] - OPPOSITE[slot])

    target = [landing(s) for s in range(8)]

    def remote(src, dst, send, recv, slot):
        return pltpu.make_async_remote_copy(
            src_ref=src, dst_ref=dst, send_sem=send, recv_sem=recv,
            device_id=device(slot), device_id_type=pl.DeviceIdType.MESH,
        )

    barrier = pltpu.get_barrier_semaphore()
    for slot in range(8):
        pl.semaphore_signal(barrier, inc=1, device_id=device(slot), device_id_type=pl.DeviceIdType.MESH)

    sources = (pos_h, occ_h, nf_h, spec_h, esh_h, esc_h, rw_h, mix_h, ro_h)
    targets = (pos, occ, nf, spec, esh, esc, rw, mix, ro)
    loads = [pltpu.make_async_copy(a, b, in_sem.at[i]) for i, (a, b) in enumerate(zip(sources, targets))]
    for load in loads:
        load.start()


    for load in loads[:3]:
        load.wait()
    occ_row = occ[0].astype(F32)
    own = jnp.concatenate([pos[0, a] for a in range(3)] + [occ_row, jnp.zeros((4, S), F32)], axis=0)
    own = jnp.concatenate([own, own], axis=1)
    posb[8] = own
    columns = own.T
    occ_col = columns[0:S, 3:4]
    feat[8] = nf[0, 0] * occ_col.astype(BF16)
    feat[9] = jnp.zeros((S, C), BF16)

    pl.semaphore_wait(barrier, 8)
    def pos_copy(s, there):
        return remote(posb.at[8], posb.at[there], ps_sem.at[s], pr_sem.at[there], s)

    def feat_copy(s, there):
        return remote(feat.at[8], feat.at[there], fs_sem.at[s], fr_sem.at[there], s)

    def piece_copy(s, there):
        return remote(pieces.at[s], precv.at[there], ds_sem.at[s], dr_sem.at[there], s)

    def grad_copy(s, there):
        return remote(gsend.at[s // 2], grecv.at[there], gs_sem.at[s], gr_sem.at[there], s)

    for group in (range(3), range(3, 8)):
        for s in group:
            pos_copy(s, target[s]).start()
        for s in group:
            feat_copy(s, target[s]).start()

    for load in loads[3:]:
        load.wait()
    species = spec[0]
    shift_row = jnp.zeros((1, S), F32)
    scale_row = jnp.zeros((1, S), F32)
    for kind in range(esh.shape[0]):
        hit = species == kind
        shift_row = jnp.where(hit, esh[kind], shift_row)
        scale_row = jnp.where(hit, esc[kind], scale_row)
    low = lax.broadcasted_iota(jnp.int32, (1, C), 1) < S
    for a in range(3):
        cols[a] = jnp.broadcast_to(columns[0:S, a : a + 1], (S, C))
    scale_tile = jnp.concatenate([scale_row, jnp.zeros((7, S), F32)], axis=0)
    scale_col = jnp.concatenate([scale_tile, scale_tile], axis=1).T[0:S, 0:1]
    coef_col = occ_col * scale_col

    def pair_tile(tile, own_tile):
        lanes = pl.ds(tile * C, C)

        def body(ib, carry):
            at = pl.ds(pl.multiple_of(ib * 16, 16), 16)
            centre = [cols[a, at, :] for a in range(3)]
            other = [rows[a : a + 1, lanes] for a in range(3)]
            eye = None
            if own_tile:
                sub = lax.broadcasted_iota(jnp.int32, (16, C), 0) + ib * 16
                eye = (sub == lax.broadcasted_iota(jnp.int32, (16, C), 1)).astype(F32)
            radial, dradial, u, rinv = geometry(centre, other, eye)
            for n in range(NB):
                geo[n, at, lanes] = radial[n]
                geo[NB + n, at, lanes] = dradial[n]
            for a in range(3):
                geo[2 * NB + a, at, lanes] = u[a]
            geo[2 * NB + 3, at, lanes] = rinv
            ys = harmonics(u)
            for n in range(NB):
                for lm in range(9):
                    value = radial[n] if lm == 0 else radial[n] * ys[lm]
                    basis[pl.ds(pl.multiple_of((n * 9 + lm) * S + ib * 16, 16), 16), lanes] = value.astype(BF16)
            return carry

        lax.fori_loop(0, 4, body, 0, unroll=True)

    for a in range(3):
        rows[a : a + 1, pl.ds(4 * C, C)] = jnp.where(low, posb[8, a : a + 1, :], FAR)
    pair_tile(4, True)

    def neighbour_tile(tile):
        for s in (2 * tile, 2 * tile + 1):
            pos_copy(s, s).wait_recv()
        first, second = OFFSETS[2 * tile], OFFSETS[2 * tile + 1]
        for a in range(3):
            pair = jnp.where(low, posb[2 * tile, a : a + 1, :], posb[2 * tile + 1, a : a + 1, :])
            if a == 0:
                pair = pair + jnp.where(low, SIDE * first[0], SIDE * second[0])
            if a == 1:
                pair = pair + jnp.where(low, SIDE * first[1], SIDE * second[1]) * flip.astype(F32)
            rows[a : a + 1, pl.ds(tile * C, C)] = pair
        pair_tile(tile, False)

    neighbour_tile(3)
    neighbour_tile(2)
    for s in (7, 6, 5, 4):
        feat_copy(s, s).wait_recv()
    near[...] = jnp.dot(
        basis[:, pl.ds(2 * C, 3 * C)], feat[4:10].reshape(6 * S, C), preferred_element_type=F32
    )
    neighbour_tile(1)
    neighbour_tile(0)
    for s in (3, 2, 1, 0):
        feat_copy(s, s).wait_recv()
    sums = near[...] + jnp.dot(
        basis[:, pl.ds(0, 2 * C)], feat[0:4].reshape(4 * S, C), preferred_element_type=F32
    )
    weight = [[rw[d, n : n + 1, :] for d in range(3)] for n in range(NB)]
    amp = []
    for lm in range(9):
        total = None
        for n in range(NB):
            k = n * 9 + lm
            term = weight[n][DEGREE[lm]] * sums[k * S : (k + 1) * S]
            total = term if total is None else total + term
        amp.append(total)
    second = amp[1] * amp[1] + amp[2] * amp[2] + amp[3] * amp[3]
    third = amp[4] * amp[4] + amp[5] * amp[5] + amp[6] * amp[6] + amp[7] * amp[7] + amp[8] * amp[8]
    invariants = jnp.concatenate([amp[0].astype(BF16), second.astype(BF16), third.astype(BF16)], axis=1)
    pre = jnp.dot(invariants, mix[...], preferred_element_type=F32)
    sigma = jax.nn.sigmoid(pre)
    readout = ro[...]
    dpre = (coef_col * readout * sigma * (1.0 + pre * (1.0 - sigma))).astype(BF16)
    dinv = lax.dot_general(dpre, mix[...], (((1,), (1,)), ((), ())), preferred_element_type=F32)
    for lm in range(9):
        d = DEGREE[lm]
        damp = dinv[:, d * C : (d + 1) * C]
        if d > 0:
            damp = 2.0 * amp[lm] * damp
        for n in range(NB):
            coeff[pl.ds((n * 9 + lm) * S, S), :] = (weight[n][d] * damp).astype(BF16)
    for k in range(K // 2):
        coeff_t[:, pl.ds(k * C, C)] = coeff[pl.ds(k * C, C), :].T

    def force_tile(tile, column):
        lanes = pl.ds(tile * C, C)

        def body(ib, carry):
            at = pl.ds(pl.multiple_of(ib * 16, 16), 16)
            radial = [geo[n, at, lanes] for n in range(NB)]
            dradial = [geo[NB + n, at, lanes] for n in range(NB)]
            u = [geo[2 * NB + a, at, lanes] for a in range(3)]
            rinv = geo[2 * NB + 3, at, lanes]
            ys = harmonics(u)
            along = [None] * NB
            across = [None] * 9
            for n in range(NB):
                for lm in range(9):
                    value = dbs[pl.ds(pl.multiple_of((n * 9 + lm) * S + ib * 16, 16), 16), pl.ds(column, C)]
                    term = value if lm == 0 else value * ys[lm]
                    along[n] = term if along[n] is None else along[n] + term
                    if lm:
                        term = radial[n] * value
                        across[lm] = term if across[lm] is None else across[lm] + term
            outward = along[0] * dradial[0]
            for n in range(1, NB):
                outward = outward + along[n] * dradial[n]
            e = across
            ux, uy, uz = u
            vx = R3 * e[1] + R15 * (uy * e[4] + uz * e[7] + ux * e[8])
            vy = R3 * e[2] + R15 * (ux * e[4] + uz * e[5] - uy * e[8])
            vz = R3 * e[3] + R15 * (uy * e[5] + ux * e[7]) + (3.0 * R5) * (uz * e[6])
            radial_part = outward - rinv * (ux * vx + uy * vy + uz * vz)
            sums_j = []
            for a, v in enumerate((vx, vy, vz)):
                grad = rinv * v + u[a] * radial_part
                if tile == 0:
                    giacc[a, at, :] = grad
                else:
                    giacc[a, at, :] = giacc[a, at, :] + grad
                sums_j.append(carry[a] + grad[0:8] + grad[8:16])
            return tuple(sums_j)

        zero = jnp.zeros((8, C), F32)
        totals = lax.fori_loop(0, 4, body, (zero, zero, zero), unroll=True)
        return jnp.concatenate(
            [jnp.sum(t, axis=0, keepdims=True) for t in totals] + [jnp.zeros((5, C), F32)], axis=0
        )

    def feature_part(lanes):
        return jnp.dot(coeff_t[...], basis[:, lanes], preferred_element_type=F32).T

    for half in range(2):
        dbs[...] = lax.dot_general(
            coeff[...], feat[half * 4 : half * 4 + 4].reshape(4 * S, C), (((1,), (1,)), ((), ())), preferred_element_type=F32
        )
        part = feature_part(pl.ds(half * 2 * C, 2 * C)).astype(BF16)
        for i in range(4):
            s = half * 4 + i
            pieces[s] = part[i * S : (i + 1) * S]
            piece_copy(s, target[s]).start()
        for i in range(2):
            tile = half * 2 + i
            gsend[tile] = force_tile(tile, i * C)
            for s in (2 * tile, 2 * tile + 1):
                grad_copy(s, target[s]).start()

    own_part = feature_part(pl.ds(4 * C, C))
    dbs[:, pl.ds(0, C)] = lax.dot_general(
        coeff[...], feat[8:10].reshape(2 * S, C), (((1,), (1,)), ((), ())), preferred_element_type=F32
    )
    own_grad = force_tile(4, 0)
    centre_rows = [jnp.sum(giacc[a].T, axis=0, keepdims=True) for a in range(3)]
    energy_row = jnp.sum((pre * sigma * readout).T, axis=0, keepdims=True)
    energy_o[0] = occ_row * (shift_row + scale_row * energy_row)

    gathered = own_part[:S, :]
    for s in (7, 6, 5, 4, 3, 2, 1, 0):
        piece_copy(s, s).wait_recv()
        gathered = gathered + precv[s].astype(F32)
    fgrad_o[0, 0] = gathered * occ_col

    for s in range(8):
        grad_copy(s, s).wait_recv()
    upper = grecv[0] + grecv[3] + grecv[4] + grecv[7]
    lower = grecv[1] + grecv[2] + grecv[5] + grecv[6] + own_grad
    back = lower[0:3, 0:S] + upper[0:3, S:C]
    for a in range(3):
        force_o[0, a] = centre_rows[a] - back[a : a + 1]

    for s in range(8):
        for copy in (pos_copy, feat_copy, piece_copy, grad_copy):
            copy(s, target[s]).wait_send()


def emit(a, b, c, ao, bo, co, sem):
    copies = [pltpu.make_async_copy(x, y, sem.at[i]) for i, (x, y) in enumerate(((a, ao), (b, bo), (c, co)))]
    for copy in copies:
        copy.start()
    for copy in copies:
        copy.wait()


def shards(nf, pos, spec, occ, esh, esc, rw, mix, ro):
    vmem = pl.BlockSpec(memory_space=pltpu.VMEM)
    hbm = pl.BlockSpec(memory_space=pltpu.HBM)
    dma = pltpu.SemaphoreType.DMA((8,))
    shapes = (
        jax.ShapeDtypeStruct((1, 1, S), F32),
        jax.ShapeDtypeStruct((1, 3, 1, S), F32),
        jax.ShapeDtypeStruct((1, 1, S, C), F32),
    )
    inputs = (nf.swapaxes(2, 3), pos.swapaxes(1, 2), spec, occ, esh, esc, rw.swapaxes(0, 1), mix, ro.reshape(1, C))
    results = pl.pallas_call(
        kernel,
        out_shape=shapes,
        in_specs=[hbm] * 9,
        out_specs=(vmem, vmem, vmem),
        scratch_shapes=[
            pltpu.VMEM((1, 1, S, C), BF16),
            pltpu.VMEM((1, 3, 1, S), F32),
            pltpu.VMEM((1, 1, S), jnp.int32),
            pltpu.VMEM((1, 1, S), jnp.int32),
            pltpu.SMEM(esh.shape, F32),
            pltpu.SMEM(esh.shape, F32),
            pltpu.VMEM((3, NB, C), F32),
            pltpu.VMEM((3 * C, C), BF16),
            pltpu.VMEM((1, C), F32),
            pltpu.VMEM((10, S, C), BF16),
            pltpu.VMEM((9, 8, C), F32),
            pltpu.VMEM((8, LANES), F32),
            pltpu.VMEM((3, S, C), F32),
            pltpu.VMEM((K * S, LANES), BF16),
            pltpu.VMEM((3 * NB, S, LANES), F32),
            pltpu.VMEM((K * S, 2 * C), F32),
            pltpu.VMEM((K * S, C), BF16),
            pltpu.VMEM((C, K * S), BF16),
            pltpu.VMEM((K * S, C), F32),
            pltpu.VMEM((8, S, C), BF16),
            pltpu.VMEM((4, 8, C), F32),
            pltpu.VMEM((8, S, C), BF16),
            pltpu.VMEM((8, 8, C), F32),
            pltpu.VMEM((3, S, C), F32),
            dma, dma, dma, dma, dma, dma, dma, dma,
            pltpu.SemaphoreType.DMA((9,)),
        ],
        compiler_params=pltpu.CompilerParams(
            collective_id=0, has_side_effects=True, vmem_limit_bytes=48 * 1024 * 1024
        ),
        cost_estimate=pl.CostEstimate(flops=1_100_000_000, bytes_accessed=400_000, transcendentals=100_000),
    )(*[pltpu.with_memory_space_constraint(v, pltpu.HBM) for v in inputs])
    energy, forces, fgrad = pl.pallas_call(
        emit,
        out_shape=shapes,
        in_specs=[vmem] * 3,
        out_specs=(hbm,) * 3,
        scratch_shapes=[pltpu.SemaphoreType.DMA((3,))],
        compiler_params=pltpu.CompilerParams(vmem_limit_bytes=1024 * 1024),
    )(*results)
    return energy, forces.swapaxes(1, 2), fgrad.swapaxes(2, 3)


def solution(mesh):
    placed = (
        P("gx", "gy", None, None),
        P("gx", "gy", None, None),
        P("gx", "gy", None),
        P("gx", "gy", None),
        P(), P(), P(), P(), P(),
    )
    return jax.shard_map(
        shards,
        mesh=mesh,
        in_specs=placed,
        out_specs=(P("gx", "gy", None), P("gx", "gy", None, None), P("gx", "gy", None, None)),
        check_vma=False,
    )
```

```python
import math

import jax
import jax.numpy as jnp
from jax import lax
from jax.experimental import pallas as pl
from jax.experimental.pallas import tpu as pltpu
from jax.sharding import PartitionSpec as P

NB = 4
SIDE = 5.0
OFFSETS = ((-1, 1), (1, 1), (0, 1), (1, 0), (-1, -1), (1, -1), (0, -1), (-1, 0))
OPPOSITE = (5, 4, 6, 7, 1, 0, 2, 3)
MIRROR = (1, 0, 2, 7, 5, 4, 6, 3)
DEGREE = (0, 1, 1, 1, 2, 2, 2, 2, 2)
S, C, K = 64, 128, 36
LANES = 640
FAR = 1.0e4

SIN_POLY = (0.9999999535014531, -4.934792863930696, 4.058412034401939, -1.331881022938153, 0.21969869886953738)
COS_POLY = (3.1415925800860727, -5.167706881428528, 2.5500314173387735, -0.5980454081793043, 0.07722057976690203)
R3, R5, R15 = math.sqrt(3.0), math.sqrt(5.0), math.sqrt(15.0)
F32, BF16 = jnp.float32, jnp.bfloat16


def poly(coefs, x):
    total = coefs[-1]
    for coef in coefs[-2::-1]:
        total = total * x + coef
    return total


def geometry(centre, other, eye):
    rx, ry, rz = (o - c for o, c in zip(other, centre))
    dist_sq = rx * rx + ry * ry + rz * rz
    if eye is not None:
        dist_sq = dist_sq + eye
    rinv = lax.rsqrt(dist_sq)
    x = jnp.minimum(dist_sq * rinv * (1.0 / SIDE), 1.0)
    y = x - 0.5
    y2 = y * y
    s1 = poly(SIN_POLY, y2)
    c1 = -y * poly(COS_POLY, y2)
    x2 = x * x
    x5 = x2 * x2 * x
    env = 1.0 + x5 * x * (-28.0 + x * (48.0 - 21.0 * x))
    denv = x5 * (-168.0 + x * (336.0 - 168.0 * x))
    norm = math.sqrt(2.0 / SIDE)
    kinv = norm * rinv
    if eye is not None:
        kinv = kinv * (1.0 - eye)
    g = env * kinv
    dg = denv * kinv * (1.0 / SIDE) - g * rinv
    t = 2.0 * c1
    sines = [s1, t * s1]
    cosines = [c1, t * c1 - 1.0]
    for _ in range(NB - 2):
        sines.append(t * sines[-1] - sines[-2])
        cosines.append(t * cosines[-1] - cosines[-2])
    radial = [g * s for s in sines]
    dradial = [dg * s + (g * ((n + 1) * math.pi / SIDE)) * c for n, (s, c) in enumerate(zip(sines, cosines))]
    return radial, dradial, (rx * rinv, ry * rinv, rz * rinv), rinv


def harmonics(u):
    ux, uy, uz = u
    ax, ay, az = R3 * ux, R3 * uy, R3 * uz
    bx, by = R5 * ax, R5 * ay
    return (
        None,
        ax,
        ay,
        az,
        bx * uy,
        by * uz,
        (1.5 * R5) * (uz * uz) - 0.5 * R5,
        bx * uz,
        0.5 * (bx * ux - by * uy),
    )


def kernel(
    nf_h, pos_h, spec_h, occ_h, esh_h, esc_h, rw_h, mix_h, ro_h,
    energy_o, force_o, fgrad_o,
    nf, pos, spec, occ, esh, esc, rw, mix, ro,
    feat, posb, rows, cols, basis, geo, dbs, coeff, coeff_t, near, pieces, gsend, precv, grecv, giacc,
    ps_sem, pr_sem, fs_sem, fr_sem, ds_sem, dr_sem, gs_sem, gr_sem, in_sem,
):
    nx, ny = lax.axis_size("gx"), lax.axis_size("gy")
    mx, my = lax.axis_index("gx"), lax.axis_index("gy")

    def wrapped(index, step, count):
        index = index + step
        index = jnp.where(index < 0, index + count, index)
        return jnp.where(index >= count, index - count, index)

    first_column = my == 0
    flip = jnp.where(first_column, -1, 1)

    def device(slot):
        p, q = OFFSETS[slot]
        return (wrapped(mx, p, nx) if p else mx, wrapped(my, q * flip, ny) if q else my)

    def landing(slot):
        if OFFSETS[slot][1] == 0:
            return OPPOSITE[slot]
        mixed = jnp.logical_xor(first_column, device(slot)[1] == 0)
        return jnp.where(mixed, MIRROR[slot], OPPOSITE[slot])

    target = [landing(s) for s in range(8)]

    def remote(src, dst, send, recv, slot):
        return pltpu.make_async_remote_copy(
            src_ref=src, dst_ref=dst, send_sem=send, recv_sem=recv,
            device_id=device(slot), device_id_type=pl.DeviceIdType.MESH,
        )

    barrier = pltpu.get_barrier_semaphore()
    for slot in range(8):
        pl.semaphore_signal(barrier, inc=1, device_id=device(slot), device_id_type=pl.DeviceIdType.MESH)

    sources = (pos_h, occ_h, nf_h, spec_h, esh_h, esc_h, rw_h, mix_h, ro_h)
    targets = (pos, occ, nf, spec, esh, esc, rw, mix, ro)
    loads = [pltpu.make_async_copy(a, b, in_sem.at[i]) for i, (a, b) in enumerate(zip(sources, targets))]
    for load in loads:
        load.start()


    for load in loads[:3]:
        load.wait()
    occ_row = occ[0].astype(F32)
    own = jnp.concatenate([pos[0, a] for a in range(3)] + [occ_row, jnp.zeros((4, S), F32)], axis=0)
    own = jnp.concatenate([own, own], axis=1)
    posb[8] = own
    columns = own.T
    occ_col = columns[0:S, 3:4]
    feat[8] = nf[0, 0] * occ_col.astype(BF16)
    feat[9] = jnp.zeros((S, C), BF16)

    pl.semaphore_wait(barrier, 8)
    def pos_copy(s, there):
        return remote(posb.at[8], posb.at[there], ps_sem.at[s], pr_sem.at[there], s)

    def feat_copy(s, there):
        return remote(feat.at[8], feat.at[there], fs_sem.at[s], fr_sem.at[there], s)

    def piece_copy(s, there):
        return remote(pieces.at[s], precv.at[there], ds_sem.at[s], dr_sem.at[there], s)

    def grad_copy(s, there):
        return remote(gsend.at[s // 2], grecv.at[there], gs_sem.at[s], gr_sem.at[there], s)

    for group in (range(3), range(3, 8)):
        for s in group:
            pos_copy(s, target[s]).start()
        for s in group:
            feat_copy(s, target[s]).start()

    for load in loads[3:]:
        load.wait()
    species = spec[0]
    shift_row = jnp.zeros((1, S), F32)
    scale_row = jnp.zeros((1, S), F32)
    for kind in range(esh.shape[0]):
        hit = species == kind
        shift_row = jnp.where(hit, esh[kind], shift_row)
        scale_row = jnp.where(hit, esc[kind], scale_row)
    low = lax.broadcasted_iota(jnp.int32, (1, C), 1) < S
    for a in range(3):
        cols[a] = jnp.broadcast_to(columns[0:S, a : a + 1], (S, C))
    scale_tile = jnp.concatenate([scale_row, jnp.zeros((7, S), F32)], axis=0)
    scale_col = jnp.concatenate([scale_tile, scale_tile], axis=1).T[0:S, 0:1]
    coef_col = occ_col * scale_col

    def pair_tile(tile, own_tile):
        lanes = pl.ds(tile * C, C)

        def body(ib, carry):
            at = pl.ds(pl.multiple_of(ib * 16, 16), 16)
            centre = [cols[a, at, :] for a in range(3)]
            other = [rows[a : a + 1, lanes] for a in range(3)]
            eye = None
            if own_tile:
                sub = lax.broadcasted_iota(jnp.int32, (16, C), 0) + ib * 16
                eye = (sub == lax.broadcasted_iota(jnp.int32, (16, C), 1)).astype(F32)
            radial, dradial, u, rinv = geometry(centre, other, eye)
            for n in range(NB):
                geo[n, at, lanes] = radial[n]
                geo[NB + n, at, lanes] = dradial[n]
            for a in range(3):
                geo[2 * NB + a, at, lanes] = u[a]
            geo[2 * NB + 3, at, lanes] = rinv
            ys = harmonics(u)
            for n in range(NB):
                for lm in range(9):
                    value = radial[n] if lm == 0 else radial[n] * ys[lm]
                    basis[pl.ds(pl.multiple_of((n * 9 + lm) * S + ib * 16, 16), 16), lanes] = value.astype(BF16)
            return carry

        lax.fori_loop(0, 4, body, 0, unroll=True)

    for a in range(3):
        rows[a : a + 1, pl.ds(4 * C, C)] = jnp.where(low, posb[8, a : a + 1, :], FAR)
    pair_tile(4, True)

    def neighbour_tile(tile):
        for s in (2 * tile, 2 * tile + 1):
            pos_copy(s, s).wait_recv()
        first, second = OFFSETS[2 * tile], OFFSETS[2 * tile + 1]
        for a in range(3):
            pair = jnp.where(low, posb[2 * tile, a : a + 1, :], posb[2 * tile + 1, a : a + 1, :])
            if a == 0:
                pair = pair + jnp.where(low, SIDE * first[0], SIDE * second[0])
            if a == 1:
                pair = pair + jnp.where(low, SIDE * first[1], SIDE * second[1]) * flip.astype(F32)
            rows[a : a + 1, pl.ds(tile * C, C)] = pair
        pair_tile(tile, False)

    neighbour_tile(3)
    neighbour_tile(2)
    for s in (7, 6, 5, 4):
        feat_copy(s, s).wait_recv()
    near[...] = jnp.dot(
        basis[:, pl.ds(2 * C, 3 * C)], feat[4:10].reshape(6 * S, C), preferred_element_type=F32
    )
    neighbour_tile(1)
    neighbour_tile(0)
    for s in (3, 2, 1, 0):
        feat_copy(s, s).wait_recv()
    sums = near[...] + jnp.dot(
        basis[:, pl.ds(0, 2 * C)], feat[0:4].reshape(4 * S, C), preferred_element_type=F32
    )
    weight = [[rw[d, n : n + 1, :] for d in range(3)] for n in range(NB)]
    amp = []
    for lm in range(9):
        total = None
        for n in range(NB):
            k = n * 9 + lm
            term = weight[n][DEGREE[lm]] * sums[k * S : (k + 1) * S]
            total = term if total is None else total + term
        amp.append(total)
    second = amp[1] * amp[1] + amp[2] * amp[2] + amp[3] * amp[3]
    third = amp[4] * amp[4] + amp[5] * amp[5] + amp[6] * amp[6] + amp[7] * amp[7] + amp[8] * amp[8]
    invariants = jnp.concatenate([amp[0].astype(BF16), second.astype(BF16), third.astype(BF16)], axis=1)
    pre = jnp.dot(invariants, mix[...], preferred_element_type=F32)
    sigma = jax.nn.sigmoid(pre)
    readout = ro[...]
    dpre = (coef_col * readout * sigma * (1.0 + pre * (1.0 - sigma))).astype(BF16)
    dinv = lax.dot_general(dpre, mix[...], (((1,), (1,)), ((), ())), preferred_element_type=F32)
    for lm in range(9):
        d = DEGREE[lm]
        damp = dinv[:, d * C : (d + 1) * C]
        if d > 0:
            damp = 2.0 * amp[lm] * damp
        for n in range(NB):
            coeff[pl.ds((n * 9 + lm) * S, S), :] = (weight[n][d] * damp).astype(BF16)
    for k in range(K // 2):
        coeff_t[:, pl.ds(k * C, C)] = coeff[pl.ds(k * C, C), :].T

    def force_tile(tile, column):
        lanes = pl.ds(tile * C, C)

        def body(ib, carry):
            at = pl.ds(pl.multiple_of(ib * 16, 16), 16)
            radial = [geo[n, at, lanes] for n in range(NB)]
            dradial = [geo[NB + n, at, lanes] for n in range(NB)]
            u = [geo[2 * NB + a, at, lanes] for a in range(3)]
            rinv = geo[2 * NB + 3, at, lanes]
            ys = harmonics(u)
            along = [None] * NB
            across = [None] * 9
            for n in range(NB):
                for lm in range(9):
                    value = dbs[pl.ds(pl.multiple_of((n * 9 + lm) * S + ib * 16, 16), 16), pl.ds(column, C)]
                    term = value if lm == 0 else value * ys[lm]
                    along[n] = term if along[n] is None else along[n] + term
                    if lm:
                        term = radial[n] * value
                        across[lm] = term if across[lm] is None else across[lm] + term
            outward = along[0] * dradial[0]
            for n in range(1, NB):
                outward = outward + along[n] * dradial[n]
            e = across
            ux, uy, uz = u
            vx = R3 * e[1] + R15 * (uy * e[4] + uz * e[7] + ux * e[8])
            vy = R3 * e[2] + R15 * (ux * e[4] + uz * e[5] - uy * e[8])
            vz = R3 * e[3] + R15 * (uy * e[5] + ux * e[7]) + (3.0 * R5) * (uz * e[6])
            radial_part = outward - rinv * (ux * vx + uy * vy + uz * vz)
            sums_j = []
            for a, v in enumerate((vx, vy, vz)):
                grad = rinv * v + u[a] * radial_part
                if tile == 0:
                    giacc[a, at, :] = grad
                else:
                    giacc[a, at, :] = giacc[a, at, :] + grad
                sums_j.append(carry[a] + grad[0:8] + grad[8:16])
            return tuple(sums_j)

        zero = jnp.zeros((8, C), F32)
        totals = lax.fori_loop(0, 4, body, (zero, zero, zero), unroll=True)
        return jnp.concatenate(
            [jnp.sum(t, axis=0, keepdims=True) for t in totals] + [jnp.zeros((5, C), F32)], axis=0
        )

    def feature_part(lanes):
        return jnp.dot(coeff_t[...], basis[:, lanes], preferred_element_type=F32)

    for half in range(2):
        dbs[...] = lax.dot_general(
            coeff[...], feat[half * 4 : half * 4 + 4].reshape(4 * S, C), (((1,), (1,)), ((), ())), preferred_element_type=F32
        )
        part = feature_part(pl.ds(half * 2 * C, 2 * C)).astype(BF16).T
        for i in range(4):
            s = half * 4 + i
            pieces[s] = part[i * S : (i + 1) * S]
            piece_copy(s, target[s]).start()
        for i in range(2):
            tile = half * 2 + i
            gsend[tile] = force_tile(tile, i * C)
            for s in (2 * tile, 2 * tile + 1):
                grad_copy(s, target[s]).start()

    own_part = feature_part(pl.ds(4 * C, C)).T
    dbs[:, pl.ds(0, C)] = lax.dot_general(
        coeff[...], feat[8:10].reshape(2 * S, C), (((1,), (1,)), ((), ())), preferred_element_type=F32
    )
    own_grad = force_tile(4, 0)
    centre_rows = [jnp.sum(giacc[a].T, axis=0, keepdims=True) for a in range(3)]
    energy_row = jnp.sum((pre * sigma * readout).T, axis=0, keepdims=True)
    energy_o[0] = occ_row * (shift_row + scale_row * energy_row)

    gathered = own_part[:S, :]
    for s in (7, 6, 5, 4, 3, 2, 1, 0):
        piece_copy(s, s).wait_recv()
        gathered = gathered + precv[s].astype(F32)
    fgrad_o[0, 0] = gathered * occ_col

    for s in range(8):
        grad_copy(s, s).wait_recv()
    upper = grecv[0] + grecv[3] + grecv[4] + grecv[7]
    lower = grecv[1] + grecv[2] + grecv[5] + grecv[6] + own_grad
    back = lower[0:3, 0:S] + upper[0:3, S:C]
    for a in range(3):
        force_o[0, a] = centre_rows[a] - back[a : a + 1]

    for s in range(8):
        for copy in (pos_copy, feat_copy, piece_copy, grad_copy):
            copy(s, target[s]).wait_send()


def emit(a, b, c, ao, bo, co, sem):
    copies = [pltpu.make_async_copy(x, y, sem.at[i]) for i, (x, y) in enumerate(((a, ao), (b, bo), (c, co)))]
    for copy in copies:
        copy.start()
    for copy in copies:
        copy.wait()


def shards(nf, pos, spec, occ, esh, esc, rw, mix, ro):
    vmem = pl.BlockSpec(memory_space=pltpu.VMEM)
    hbm = pl.BlockSpec(memory_space=pltpu.HBM)
    dma = pltpu.SemaphoreType.DMA((8,))
    shapes = (
        jax.ShapeDtypeStruct((1, 1, S), F32),
        jax.ShapeDtypeStruct((1, 3, 1, S), F32),
        jax.ShapeDtypeStruct((1, 1, S, C), F32),
    )
    inputs = (nf.swapaxes(2, 3), pos.swapaxes(1, 2), spec, occ, esh, esc, rw.swapaxes(0, 1), mix, ro.reshape(1, C))
    results = pl.pallas_call(
        kernel,
        out_shape=shapes,
        in_specs=[hbm] * 9,
        out_specs=(vmem, vmem, vmem),
        scratch_shapes=[
            pltpu.VMEM((1, 1, S, C), BF16),
            pltpu.VMEM((1, 3, 1, S), F32),
            pltpu.VMEM((1, 1, S), jnp.int32),
            pltpu.VMEM((1, 1, S), jnp.int32),
            pltpu.SMEM(esh.shape, F32),
            pltpu.SMEM(esh.shape, F32),
            pltpu.VMEM((3, NB, C), F32),
            pltpu.VMEM((3 * C, C), BF16),
            pltpu.VMEM((1, C), F32),
            pltpu.VMEM((10, S, C), BF16),
            pltpu.VMEM((9, 8, C), F32),
            pltpu.VMEM((8, LANES), F32),
            pltpu.VMEM((3, S, C), F32),
            pltpu.VMEM((K * S, LANES), BF16),
            pltpu.VMEM((3 * NB, S, LANES), F32),
            pltpu.VMEM((K * S, 2 * C), F32),
            pltpu.VMEM((K * S, C), BF16),
            pltpu.VMEM((C, K * S), BF16),
            pltpu.VMEM((K * S, C), F32),
            pltpu.VMEM((8, S, C), BF16),
            pltpu.VMEM((4, 8, C), F32),
            pltpu.VMEM((8, S, C), BF16),
            pltpu.VMEM((8, 8, C), F32),
            pltpu.VMEM((3, S, C), F32),
            dma, dma, dma, dma, dma, dma, dma, dma,
            pltpu.SemaphoreType.DMA((9,)),
        ],
        compiler_params=pltpu.CompilerParams(
            collective_id=0, has_side_effects=True, vmem_limit_bytes=48 * 1024 * 1024
        ),
        cost_estimate=pl.CostEstimate(flops=1_100_000_000, bytes_accessed=400_000, transcendentals=100_000),
    )(*[pltpu.with_memory_space_constraint(v, pltpu.HBM) for v in inputs])
    energy, forces, fgrad = pl.pallas_call(
        emit,
        out_shape=shapes,
        in_specs=[vmem] * 3,
        out_specs=(hbm,) * 3,
        scratch_shapes=[pltpu.SemaphoreType.DMA((3,))],
        compiler_params=pltpu.CompilerParams(vmem_limit_bytes=1024 * 1024),
    )(*results)
    return energy, forces.swapaxes(1, 2), fgrad.swapaxes(2, 3)


def solution(mesh):
    placed = (
        P("gx", "gy", None, None),
        P("gx", "gy", None, None),
        P("gx", "gy", None),
        P("gx", "gy", None),
        P(), P(), P(), P(), P(),
    )
    return jax.shard_map(
        shards,
        mesh=mesh,
        in_specs=placed,
        out_specs=(P("gx", "gy", None), P("gx", "gy", None, None), P("gx", "gy", None, None)),
        check_vma=False,
    )
```

```python
import math

import jax
import jax.numpy as jnp
from jax import lax
from jax.experimental import pallas as pl
from jax.experimental.pallas import tpu as pltpu
from jax.sharding import PartitionSpec as P

NB = 4
SIDE = 5.0
OFFSETS = ((-1, 1), (1, 1), (0, 1), (1, 0), (-1, -1), (1, -1), (0, -1), (-1, 0))
OPPOSITE = (5, 4, 6, 7, 1, 0, 2, 3)
MIRROR = (1, 0, 2, 7, 5, 4, 6, 3)
DEGREE = (0, 1, 1, 1, 2, 2, 2, 2, 2)
S, C, K = 64, 128, 36
LANES = 640
FAR = 1.0e4

SIN_POLY = (0.9999999535014531, -4.934792863930696, 4.058412034401939, -1.331881022938153, 0.21969869886953738)
COS_POLY = (3.1415925800860727, -5.167706881428528, 2.5500314173387735, -0.5980454081793043, 0.07722057976690203)
R3, R5, R15 = math.sqrt(3.0), math.sqrt(5.0), math.sqrt(15.0)
F32, BF16 = jnp.float32, jnp.bfloat16


def poly(coefs, x):
    total = coefs[-1]
    for coef in coefs[-2::-1]:
        total = total * x + coef
    return total


def geometry(centre, other, eye):
    rx, ry, rz = (o - c for o, c in zip(other, centre))
    dist_sq = rx * rx + ry * ry + rz * rz
    if eye is not None:
        dist_sq = dist_sq + eye
    rinv = lax.rsqrt(dist_sq)
    x = jnp.minimum(dist_sq * rinv * (1.0 / SIDE), 1.0)
    y = x - 0.5
    y2 = y * y
    s1 = poly(SIN_POLY, y2)
    c1 = -y * poly(COS_POLY, y2)
    x2 = x * x
    x5 = x2 * x2 * x
    env = 1.0 + x5 * x * (-28.0 + x * (48.0 - 21.0 * x))
    denv = x5 * (-168.0 + x * (336.0 - 168.0 * x))
    norm = math.sqrt(2.0 / SIDE)
    kinv = norm * rinv
    if eye is not None:
        kinv = kinv * (1.0 - eye)
    g = env * kinv
    dg = denv * kinv * (1.0 / SIDE) - g * rinv
    t = 2.0 * c1
    sines = [s1, t * s1]
    cosines = [c1, t * c1 - 1.0]
    for _ in range(NB - 2):
        sines.append(t * sines[-1] - sines[-2])
        cosines.append(t * cosines[-1] - cosines[-2])
    radial = [g * s for s in sines]
    dradial = [dg * s + (g * ((n + 1) * math.pi / SIDE)) * c for n, (s, c) in enumerate(zip(sines, cosines))]
    return radial, dradial, (rx * rinv, ry * rinv, rz * rinv), rinv


def harmonics(u):
    ux, uy, uz = u
    ax, ay, az = R3 * ux, R3 * uy, R3 * uz
    bx, by = R5 * ax, R5 * ay
    return (
        None,
        ax,
        ay,
        az,
        bx * uy,
        by * uz,
        (1.5 * R5) * (uz * uz) - 0.5 * R5,
        bx * uz,
        0.5 * (bx * ux - by * uy),
    )


def kernel(
    nf_h, pos_h, spec_h, occ_h, esh_h, esc_h, rw_h, mix_h, ro_h,
    energy_o, force_o, fgrad_o,
    nf, pos, spec, occ, esh, esc, rw, mix, ro,
    feat, posb, rows, cols, basis, geo, dbs, coeff, coeff_t, mix_t, feat_t, near, pieces, gsend, precv, grecv, giacc,
    ps_sem, pr_sem, fs_sem, fr_sem, ds_sem, dr_sem, gs_sem, gr_sem, in_sem,
):
    nx, ny = lax.axis_size("gx"), lax.axis_size("gy")
    mx, my = lax.axis_index("gx"), lax.axis_index("gy")

    def wrapped(index, step, count):
        index = index + step
        index = jnp.where(index < 0, index + count, index)
        return jnp.where(index >= count, index - count, index)

    first_column = my == 0
    flip = jnp.where(first_column, -1, 1)

    def device(slot):
        p, q = OFFSETS[slot]
        return (wrapped(mx, p, nx) if p else mx, wrapped(my, q * flip, ny) if q else my)

    def landing(slot):
        if OFFSETS[slot][1] == 0:
            return OPPOSITE[slot]
        mixed = jnp.logical_xor(first_column, device(slot)[1] == 0)
        return jnp.where(mixed, MIRROR[slot], OPPOSITE[slot])

    target = [landing(s) for s in range(8)]

    def remote(src, dst, send, recv, slot):
        return pltpu.make_async_remote_copy(
            src_ref=src, dst_ref=dst, send_sem=send, recv_sem=recv,
            device_id=device(slot), device_id_type=pl.DeviceIdType.MESH,
        )

    barrier = pltpu.get_barrier_semaphore()
    for slot in range(8):
        pl.semaphore_signal(barrier, inc=1, device_id=device(slot), device_id_type=pl.DeviceIdType.MESH)

    sources = (pos_h, occ_h, nf_h, spec_h, esh_h, esc_h, rw_h, mix_h, ro_h)
    targets = (pos, occ, nf, spec, esh, esc, rw, mix, ro)
    loads = [pltpu.make_async_copy(a, b, in_sem.at[i]) for i, (a, b) in enumerate(zip(sources, targets))]
    for load in loads:
        load.start()


    for load in loads[:3]:
        load.wait()
    occ_row = occ[0].astype(F32)
    own = jnp.concatenate([pos[0, a] for a in range(3)] + [occ_row, jnp.zeros((4, S), F32)], axis=0)
    own = jnp.concatenate([own, own], axis=1)
    posb[8] = own
    columns = own.T
    occ_col = columns[0:S, 3:4]
    feat[8] = nf[0, 0] * occ_col.astype(BF16)
    feat[9] = jnp.zeros((S, C), BF16)

    pl.semaphore_wait(barrier, 8)
    def pos_copy(s, there):
        return remote(posb.at[8], posb.at[there], ps_sem.at[s], pr_sem.at[there], s)

    def feat_copy(s, there):
        return remote(feat.at[8], feat.at[there], fs_sem.at[s], fr_sem.at[there], s)

    def piece_copy(s, there):
        return remote(pieces.at[s], precv.at[there], ds_sem.at[s], dr_sem.at[there], s)

    def grad_copy(s, there):
        return remote(gsend.at[s // 2], grecv.at[there], gs_sem.at[s], gr_sem.at[there], s)

    for group in (range(3), range(3, 8)):
        for s in group:
            pos_copy(s, target[s]).start()
        for s in group:
            feat_copy(s, target[s]).start()

    for load in loads[3:]:
        load.wait()
    species = spec[0]
    shift_row = jnp.zeros((1, S), F32)
    scale_row = jnp.zeros((1, S), F32)
    for kind in range(esh.shape[0]):
        hit = species == kind
        shift_row = jnp.where(hit, esh[kind], shift_row)
        scale_row = jnp.where(hit, esc[kind], scale_row)
    low = lax.broadcasted_iota(jnp.int32, (1, C), 1) < S
    for a in range(3):
        cols[a] = jnp.broadcast_to(columns[0:S, a : a + 1], (S, C))
    scale_tile = jnp.concatenate([scale_row, jnp.zeros((7, S), F32)], axis=0)
    scale_col = jnp.concatenate([scale_tile, scale_tile], axis=1).T[0:S, 0:1]
    coef_col = occ_col * scale_col

    def pair_tile(tile, own_tile):
        lanes = pl.ds(tile * C, C)

        def body(ib, carry):
            at = pl.ds(pl.multiple_of(ib * 16, 16), 16)
            centre = [cols[a, at, :] for a in range(3)]
            other = [rows[a : a + 1, lanes] for a in range(3)]
            eye = None
            if own_tile:
                sub = lax.broadcasted_iota(jnp.int32, (16, C), 0) + ib * 16
                eye = (sub == lax.broadcasted_iota(jnp.int32, (16, C), 1)).astype(F32)
            radial, dradial, u, rinv = geometry(centre, other, eye)
            for n in range(NB):
                geo[n, at, lanes] = radial[n]
                geo[NB + n, at, lanes] = dradial[n]
            for a in range(3):
                geo[2 * NB + a, at, lanes] = u[a]
            geo[2 * NB + 3, at, lanes] = rinv
            ys = harmonics(u)
            for n in range(NB):
                for lm in range(9):
                    value = radial[n] if lm == 0 else radial[n] * ys[lm]
                    basis[pl.ds(pl.multiple_of((n * 9 + lm) * S + ib * 16, 16), 16), lanes] = value.astype(BF16)
            return carry

        lax.fori_loop(0, 4, body, 0, unroll=True)

    for a in range(3):
        rows[a : a + 1, pl.ds(4 * C, C)] = jnp.where(low, posb[8, a : a + 1, :], FAR)
    pair_tile(4, True)

    def neighbour_tile(tile):
        for s in (2 * tile, 2 * tile + 1):
            pos_copy(s, s).wait_recv()
        first, second = OFFSETS[2 * tile], OFFSETS[2 * tile + 1]
        for a in range(3):
            pair = jnp.where(low, posb[2 * tile, a : a + 1, :], posb[2 * tile + 1, a : a + 1, :])
            if a == 0:
                pair = pair + jnp.where(low, SIDE * first[0], SIDE * second[0])
            if a == 1:
                pair = pair + jnp.where(low, SIDE * first[1], SIDE * second[1]) * flip.astype(F32)
            rows[a : a + 1, pl.ds(tile * C, C)] = pair
        pair_tile(tile, False)

    mix_t[...] = mix[...].T

    neighbour_tile(3)
    neighbour_tile(2)
    for s in (7, 6, 5, 4):
        feat_copy(s, s).wait_recv()
    near[...] = jnp.dot(
        basis[:, pl.ds(2 * C, 3 * C)], feat[4:10].reshape(6 * S, C), preferred_element_type=F32
    )
    for tile in (2, 3, 4):
        feat_t[:, pl.ds(tile * C, C)] = feat[2 * tile : 2 * tile + 2].reshape(C, C).T
    neighbour_tile(1)
    neighbour_tile(0)
    for s in (3, 2, 1, 0):
        feat_copy(s, s).wait_recv()
    sums = near[...] + jnp.dot(
        basis[:, pl.ds(0, 2 * C)], feat[0:4].reshape(4 * S, C), preferred_element_type=F32
    )
    for tile in (0, 1):
        feat_t[:, pl.ds(tile * C, C)] = feat[2 * tile : 2 * tile + 2].reshape(C, C).T
    weight = [[rw[d, n : n + 1, :] for d in range(3)] for n in range(NB)]
    amp = []
    for lm in range(9):
        total = None
        for n in range(NB):
            k = n * 9 + lm
            term = weight[n][DEGREE[lm]] * sums[k * S : (k + 1) * S]
            total = term if total is None else total + term
        amp.append(total)
    second = amp[1] * amp[1] + amp[2] * amp[2] + amp[3] * amp[3]
    third = amp[4] * amp[4] + amp[5] * amp[5] + amp[6] * amp[6] + amp[7] * amp[7] + amp[8] * amp[8]
    invariants = jnp.concatenate([amp[0].astype(BF16), second.astype(BF16), third.astype(BF16)], axis=1)
    pre = jnp.dot(invariants, mix[...], preferred_element_type=F32)
    sigma = jax.nn.sigmoid(pre)
    readout = ro[...]
    dpre = (coef_col * readout * sigma * (1.0 + pre * (1.0 - sigma))).astype(BF16)
    dinv = jnp.dot(dpre, mix_t[...], preferred_element_type=F32)
    for lm in range(9):
        d = DEGREE[lm]
        damp = dinv[:, d * C : (d + 1) * C]
        if d > 0:
            damp = 2.0 * amp[lm] * damp
        for n in range(NB):
            coeff[pl.ds((n * 9 + lm) * S, S), :] = (weight[n][d] * damp).astype(BF16)
    for k in range(K // 2):
        coeff_t[:, pl.ds(k * C, C)] = coeff[pl.ds(k * C, C), :].T

    def force_tile(tile, column):
        lanes = pl.ds(tile * C, C)

        def body(ib, carry):
            at = pl.ds(pl.multiple_of(ib * 16, 16), 16)
            radial = [geo[n, at, lanes] for n in range(NB)]
            dradial = [geo[NB + n, at, lanes] for n in range(NB)]
            u = [geo[2 * NB + a, at, lanes] for a in range(3)]
            rinv = geo[2 * NB + 3, at, lanes]
            ys = harmonics(u)
            along = [None] * NB
            across = [None] * 9
            for n in range(NB):
                for lm in range(9):
                    value = dbs[pl.ds(pl.multiple_of((n * 9 + lm) * S + ib * 16, 16), 16), pl.ds(column, C)]
                    term = value if lm == 0 else value * ys[lm]
                    along[n] = term if along[n] is None else along[n] + term
                    if lm:
                        term = radial[n] * value
                        across[lm] = term if across[lm] is None else across[lm] + term
            outward = along[0] * dradial[0]
            for n in range(1, NB):
                outward = outward + along[n] * dradial[n]
            e = across
            ux, uy, uz = u
            vx = R3 * e[1] + R15 * (uy * e[4] + uz * e[7] + ux * e[8])
            vy = R3 * e[2] + R15 * (ux * e[4] + uz * e[5] - uy * e[8])
            vz = R3 * e[3] + R15 * (uy * e[5] + ux * e[7]) + (3.0 * R5) * (uz * e[6])
            radial_part = outward - rinv * (ux * vx + uy * vy + uz * vz)
            sums_j = []
            for a, v in enumerate((vx, vy, vz)):
                grad = rinv * v + u[a] * radial_part
                if tile == 0:
                    giacc[a, at, :] = grad
                else:
                    giacc[a, at, :] = giacc[a, at, :] + grad
                sums_j.append(carry[a] + grad[0:8] + grad[8:16])
            return tuple(sums_j)

        zero = jnp.zeros((8, C), F32)
        totals = lax.fori_loop(0, 4, body, (zero, zero, zero), unroll=True)
        return jnp.concatenate(
            [jnp.sum(t, axis=0, keepdims=True) for t in totals] + [jnp.zeros((5, C), F32)], axis=0
        )

    def feature_part(lanes):
        return jnp.dot(coeff_t[...], basis[:, lanes], preferred_element_type=F32)

    for half in range(2):
        dbs[...] = jnp.dot(coeff[...], feat_t[:, pl.ds(half * 2 * C, 2 * C)], preferred_element_type=F32)
        part = feature_part(pl.ds(half * 2 * C, 2 * C)).astype(BF16).T
        for i in range(4):
            s = half * 4 + i
            pieces[s] = part[i * S : (i + 1) * S]
            piece_copy(s, target[s]).start()
        for i in range(2):
            tile = half * 2 + i
            gsend[tile] = force_tile(tile, i * C)
            for s in (2 * tile, 2 * tile + 1):
                grad_copy(s, target[s]).start()

    own_part = feature_part(pl.ds(4 * C, C)).T
    dbs[:, pl.ds(0, C)] = jnp.dot(coeff[...], feat_t[:, pl.ds(4 * C, C)], preferred_element_type=F32)
    own_grad = force_tile(4, 0)
    centre_rows = [jnp.sum(giacc[a].T, axis=0, keepdims=True) for a in range(3)]
    energy_row = jnp.sum((pre * sigma * readout).T, axis=0, keepdims=True)
    energy_o[0] = occ_row * (shift_row + scale_row * energy_row)

    gathered = own_part[:S, :]
    for s in (7, 6, 5, 4, 3, 2, 1, 0):
        piece_copy(s, s).wait_recv()
        gathered = gathered + precv[s].astype(F32)
    fgrad_o[0, 0] = gathered * occ_col

    for s in range(8):
        grad_copy(s, s).wait_recv()
    upper = grecv[0] + grecv[3] + grecv[4] + grecv[7]
    lower = grecv[1] + grecv[2] + grecv[5] + grecv[6] + own_grad
    back = lower[0:3, 0:S] + upper[0:3, S:C]
    for a in range(3):
        force_o[0, a] = centre_rows[a] - back[a : a + 1]

    for s in range(8):
        for copy in (pos_copy, feat_copy, piece_copy, grad_copy):
            copy(s, target[s]).wait_send()


def emit(a, b, c, ao, bo, co, sem):
    copies = [pltpu.make_async_copy(x, y, sem.at[i]) for i, (x, y) in enumerate(((a, ao), (b, bo), (c, co)))]
    for copy in copies:
        copy.start()
    for copy in copies:
        copy.wait()


def shards(nf, pos, spec, occ, esh, esc, rw, mix, ro):
    vmem = pl.BlockSpec(memory_space=pltpu.VMEM)
    hbm = pl.BlockSpec(memory_space=pltpu.HBM)
    dma = pltpu.SemaphoreType.DMA((8,))
    shapes = (
        jax.ShapeDtypeStruct((1, 1, S), F32),
        jax.ShapeDtypeStruct((1, 3, 1, S), F32),
        jax.ShapeDtypeStruct((1, 1, S, C), F32),
    )
    inputs = (nf.swapaxes(2, 3), pos.swapaxes(1, 2), spec, occ, esh, esc, rw.swapaxes(0, 1), mix, ro.reshape(1, C))
    results = pl.pallas_call(
        kernel,
        out_shape=shapes,
        in_specs=[hbm] * 9,
        out_specs=(vmem, vmem, vmem),
        scratch_shapes=[
            pltpu.VMEM((1, 1, S, C), BF16),
            pltpu.VMEM((1, 3, 1, S), F32),
            pltpu.VMEM((1, 1, S), jnp.int32),
            pltpu.VMEM((1, 1, S), jnp.int32),
            pltpu.SMEM(esh.shape, F32),
            pltpu.SMEM(esh.shape, F32),
            pltpu.VMEM((3, NB, C), F32),
            pltpu.VMEM((3 * C, C), BF16),
            pltpu.VMEM((1, C), F32),
            pltpu.VMEM((10, S, C), BF16),
            pltpu.VMEM((9, 8, C), F32),
            pltpu.VMEM((8, LANES), F32),
            pltpu.VMEM((3, S, C), F32),
            pltpu.VMEM((K * S, LANES), BF16),
            pltpu.VMEM((3 * NB, S, LANES), F32),
            pltpu.VMEM((K * S, 2 * C), F32),
            pltpu.VMEM((K * S, C), BF16),
            pltpu.VMEM((C, K * S), BF16),
            pltpu.VMEM((C, 3 * C), BF16),
            pltpu.VMEM((C, LANES), BF16),
            pltpu.VMEM((K * S, C), F32),
            pltpu.VMEM((8, S, C), BF16),
            pltpu.VMEM((4, 8, C), F32),
            pltpu.VMEM((8, S, C), BF16),
            pltpu.VMEM((8, 8, C), F32),
            pltpu.VMEM((3, S, C), F32),
            dma, dma, dma, dma, dma, dma, dma, dma,
            pltpu.SemaphoreType.DMA((9,)),
        ],
        compiler_params=pltpu.CompilerParams(
            collective_id=0, has_side_effects=True, vmem_limit_bytes=48 * 1024 * 1024
        ),
        cost_estimate=pl.CostEstimate(flops=1_100_000_000, bytes_accessed=400_000, transcendentals=100_000),
    )(*[pltpu.with_memory_space_constraint(v, pltpu.HBM) for v in inputs])
    energy, forces, fgrad = pl.pallas_call(
        emit,
        out_shape=shapes,
        in_specs=[vmem] * 3,
        out_specs=(hbm,) * 3,
        scratch_shapes=[pltpu.SemaphoreType.DMA((3,))],
        compiler_params=pltpu.CompilerParams(vmem_limit_bytes=1024 * 1024),
    )(*results)
    return energy, forces.swapaxes(1, 2), fgrad.swapaxes(2, 3)


def solution(mesh):
    placed = (
        P("gx", "gy", None, None),
        P("gx", "gy", None, None),
        P("gx", "gy", None),
        P("gx", "gy", None),
        P(), P(), P(), P(), P(),
    )
    return jax.shard_map(
        shards,
        mesh=mesh,
        in_specs=placed,
        out_specs=(P("gx", "gy", None), P("gx", "gy", None, None), P("gx", "gy", None, None)),
        check_vma=False,
    )
```
